1024 devices in a mesh: row: 8 (over x, core), col: 128 (over y, z).
Axes of the slice: x: 4, y: 4, z: 32, core: 2. Of those that a mesh axis runs over, the one named last changes fastest.
Arguments:
- tokens: bfloat16 [2048, 8192], P('col', 'row'), may hold values from -6 to 6
- route_index: int32 [512], replicated, may hold values from 0 to 2047, as said below
- router_score: float32 [512], replicated, may hold values from 0.1 to 1
- out_grad: bfloat16 [512, 8192], P(None, 'row'), may hold values from -6 to 6
- gate_weight: bfloat16 [8192, 22016], P('row', 'col'), may hold values from -0.0625 to 0.0625
- up_weight: bfloat16 [8192, 22016], P('row', 'col'), may hold values from -0.0625 to 0.0625
- down_weight: bfloat16 [22016, 8192], P('col', 'row'), may hold values from -0.0390625 to 0.0390625
Outputs:
- d_rows: bfloat16 [512, 8192], P('col', 'row')
- d_gate: bfloat16 [8192, 22016], P('row', 'col')
- d_up: bfloat16 [8192, 22016], P('row', 'col')
- d_down: bfloat16 [22016, 8192], P('col', 'row')
The draws below stay inside these ranges and needn't reach their ends.
Inputs may be any that keep to these rules, and one draw needn't show every extreme that they name: `route_index`: the 512 entries are distinct tokens of the micro-batch; the last token is always among them.
All inputs are finite; a program needn't handle non-finite values.
Results may differ from the reference program's by a relative error of at most 0.0057.
Values may be sent and summed in bfloat16 or wider, within the bound.
No kernel may reach another device: no remote copies, remote signals or barrier semaphores. Data moves between devices by JAX's collectives and lax.ppermute only.
A program may use at most 32 MiB of HBM per device.

```python
import math
import jax
import jax.numpy as jnp
from jax import lax

D = 8192
FF = 22016
R = 512
MB = 2048


def draw_route_index(key, part):
    key = jax.random.fold_in(key, 7)
    first, second = jax.random.split(key)
    chosen = jax.random.permutation(first, MB - 1)[:R - 1].astype(jnp.int32)
    chosen = jnp.concatenate([chosen, jnp.full((1,), MB - 1, jnp.int32)])
    order = jax.random.permutation(second, R)
    return chosen[order].astype(jnp.int32)


def steps_of(key, shape, cuts, low, high):
    def one(position, parts):
        steps = jax.random.uniform(jax.random.fold_in(jax.random.fold_in(key, 6), position), (parts,), jnp.float32, low / len(cuts), high / len(cuts))
        return jnp.repeat(jnp.exp(steps), shape[position] // parts).reshape((-1,) + (1,) * (len(shape) - position - 1))

    loudness = one(*cuts[0])
    for cut in cuts[1:]:
        loudness = loudness * one(*cut)
    return loudness


def gaussian(key, shape, deviation, reach, cuts=(), held_as=jnp.bfloat16):
    array = deviation * jax.random.normal(key, shape, jnp.float32)
    if cuts:
        array = array * steps_of(key, shape, cuts, -0.22, 0.18)
    return jnp.clip(array, -reach, reach).astype(held_as)


def setup_inputs(seed: int = 0) -> dict:
    key_of = jax.random.split(jax.random.key(seed), 8)
    return {
        "tokens": gaussian(key_of[0], (MB, D), 1.0, 6.0, ((0, 128), (1, 8))),
        "route_index": draw_route_index(jax.random.fold_in(key_of[7], 71), 0),
        "router_score": jnp.clip(jnp.exp(jax.random.uniform(key_of[2], (R,), jnp.float32, math.log(0.1), math.log(1.0))), 0.1, 1.0),
        "out_grad": gaussian(key_of[3], (R, D), 1.0, 6.0, ((1, 8),)),
        "gate_weight": gaussian(key_of[4], (D, FF), D ** -0.5, 0.0625, ((0, 8), (1, 128))),
        "up_weight": gaussian(key_of[5], (D, FF), D ** -0.5, 0.0625, ((0, 8), (1, 128))),
        "down_weight": gaussian(key_of[6], (FF, D), FF ** -0.5, 0.0390625, ((0, 128), (1, 8))),
    }


def reference(tokens, route_index, router_score, out_grad, gate_weight, up_weight, down_weight):
    routed = jnp.take(tokens, route_index, axis=0)
    scaled = (router_score[:, None] * out_grad.astype(jnp.float32)).astype(jnp.bfloat16)
    gate = jnp.dot(routed, gate_weight, preferred_element_type=jnp.float32)
    up = jnp.dot(routed, up_weight, preferred_element_type=jnp.float32)
    back = lax.dot_general(scaled, down_weight, (((1,), (1,)), ((), ())), preferred_element_type=jnp.float32)
    sig = jax.nn.sigmoid(gate)
    silu = gate * sig
    hidden = (silu * up).astype(jnp.bfloat16)
    grad_up = (back * silu).astype(jnp.bfloat16)
    grad_gate = (back * up * sig * (1.0 + gate * (1.0 - sig))).astype(jnp.bfloat16)
    d_down = lax.dot_general(hidden, scaled, (((0,), (0,)), ((), ())), preferred_element_type=jnp.float32).astype(jnp.bfloat16)
    d_gate = lax.dot_general(routed, grad_gate, (((0,), (0,)), ((), ())), preferred_element_type=jnp.float32).astype(jnp.bfloat16)
    d_up = lax.dot_general(routed, grad_up, (((0,), (0,)), ((), ())), preferred_element_type=jnp.float32).astype(jnp.bfloat16)
    branch = lax.dot_general(grad_gate, gate_weight, (((1,), (1,)), ((), ())), preferred_element_type=jnp.float32)
    branch = branch + lax.dot_general(grad_up, up_weight, (((1,), (1,)), ((), ())), preferred_element_type=jnp.float32)
    d_rows = (out_grad.astype(jnp.float32) + branch).astype(jnp.bfloat16)
    return d_rows, d_gate, d_up, d_down
```

```python
import jax
import jax.numpy as jnp
from jax import lax
from jax.sharding import Mesh
from jax.sharding import PartitionSpec as P

BF = jnp.bfloat16
F32 = jnp.float32


def exchange(x, axis):
    return lax.all_to_all(x, axis, 0, 0, tiled=True)


def to_all(x, axis, count):
    return exchange(jnp.broadcast_to(x[None], (count,) + x.shape), axis)


def gather_routed(tokens, route_index):
    here, width = tokens.shape
    ny, nh, nl = lax.axis_size("y"), lax.axis_size("zh"), lax.axis_size("zl")
    quarter = width // nl
    rows = route_index.shape[0]
    cut = tokens.reshape(here, nl, quarter).transpose(1, 0, 2)
    cut = jnp.broadcast_to(cut[None], (ny, nl, here, quarter)).reshape(ny * nl, here, quarter)
    held = exchange(cut, ("y", "zl")).reshape(ny * nl * here, quarter)
    slots = rows // ny
    mine = lax.dynamic_slice_in_dim(route_index, lax.axis_index("y") * slots, slots, 0)
    owner, inner = mine // here, mine % here
    y, zh, zl = owner // (nh * nl), (owner // nl) % nh, owner % nl
    place = jnp.where(zh == lax.axis_index("zh"), (y * nl + zl) * here + inner, -1)
    pick = (place[:, None] == lax.broadcasted_iota(jnp.int32, (slots, ny * nl * here), 1)).astype(BF)
    filled = jnp.dot(pick, held, preferred_element_type=F32).astype(BF)
    each = slots // (nh * nl)
    got = exchange(filled.reshape(nh * nl, each, quarter), ("zh", "zl"))
    got = got.reshape(nh, nl, each, quarter).astype(F32).sum(0).astype(BF)
    got = jnp.broadcast_to(got[None], (nh, nl, each, quarter)).reshape(nh * nl, each, quarter)
    got = exchange(got, ("zh", "zl")).reshape(slots, quarter)
    got = to_all(got, "zl", nl).transpose(1, 0, 2).reshape(slots, width)
    return to_all(got, "y", ny).reshape(rows, width)


def activate(gate, up, back):
    sig = jax.nn.sigmoid(gate)
    silu = gate * sig
    hidden = (silu * up).astype(BF)
    grad_up = (back * silu).astype(BF)
    grad_gate = (back * up * sig * (1.0 + gate * (1.0 - sig))).astype(BF)
    return (hidden, grad_up, grad_gate)


def sum_and_activate(parts):
    nx, nc = lax.axis_size("x"), lax.axis_size("core")
    half = parts.shape[2] // nc
    core = lax.axis_index("core")
    keep = lax.dynamic_slice_in_dim(parts, core * half, half, 2)
    give = lax.dynamic_slice_in_dim(parts, (1 - core) * half, half, 2)
    chip = (keep + lax.ppermute(give, "core", [(0, 1), (1, 0)])).astype(BF)
    gate, up, back = to_all(chip, "x", nx).astype(F32).sum(0)
    out = jnp.stack(activate(gate, up, back))
    return lax.all_gather(out, "core", axis=2, tiled=True)


def scatter_rows(total, out_grad):
    rows, width = total.shape
    ny, nh, nl = lax.axis_size("y"), lax.axis_size("zh"), lax.axis_size("zl")
    slots, quarter = rows // ny, width // nl
    each = slots // (nh * nl)
    part = exchange(total.reshape(ny, slots, width), "y").astype(F32).sum(0).astype(BF)
    part = part.reshape(slots, nl, quarter).transpose(1, 0, 2)
    part = exchange(part, "zl").astype(F32).sum(0).astype(BF)
    part = exchange(part.reshape(nh * nl, each, quarter), ("zh", "zl"))
    part = part.reshape(nh, nl, each, quarter).astype(F32).sum(0)
    part = part.transpose(1, 0, 2).reshape(each, width)
    first = lax.axis_index(("y", "zh", "zl")) * each
    mine = lax.dynamic_slice_in_dim(out_grad, first, each, 0)
    return (mine.astype(F32) + part).astype(BF)


def body(tokens, route_index, router_score, out_grad, gate_weight, up_weight, down_weight):
    routed = gather_routed(tokens, route_index)
    scaled = (router_score[:, None] * out_grad.astype(F32)).astype(BF)
    dot = lambda a, b, i, j: lax.dot_general(a, b, (((i,), (j,)), ((), ())), preferred_element_type=F32)
    parts = jnp.stack(
        [
            dot(gate_weight, routed, 0, 1),
            dot(up_weight, routed, 0, 1),
            dot(down_weight, scaled, 1, 1),
        ]
    )
    hidden, grad_up, grad_gate = sum_and_activate(parts)
    d_down = dot(hidden, scaled, 1, 0).astype(BF)
    d_gate = dot(routed, grad_gate, 0, 1).astype(BF)
    d_up = dot(routed, grad_up, 0, 1).astype(BF)
    total = dot(grad_gate, gate_weight, 0, 1) + dot(grad_up, up_weight, 0, 1)
    d_rows = scatter_rows(total.astype(BF), out_grad)
    return (d_rows, d_gate, d_up, d_down)


def solution(mesh):
    rows, cols = mesh.devices.shape
    fine = Mesh(mesh.devices.reshape(rows // 2, 2, 4, cols // 16, 4), ("x", "core", "y", "zh", "zl"))
    row, col = ("x", "core"), ("y", "zh", "zl")
    placed = (
        P(col, row),
        P(),
        P(),
        P(None, row),
        P(row, col),
        P(row, col),
        P(col, row),
    )
    return jax.shard_map(
        body,
        mesh=fine,
        in_specs=placed,
        out_specs=(P(col, row), P(row, col), P(row, col), P(col, row)),
        check_vma=False,
    )
```

```python
import jax
import jax.numpy as jnp
from jax import lax
from jax.sharding import Mesh
from jax.sharding import PartitionSpec as P

BF = jnp.bfloat16
F32 = jnp.float32


def dot(a, b, i, j):
    return lax.dot_general(a, b, (((i,), (j,)), ((), ())), preferred_element_type=F32)


def exchange(x, axis):
    return lax.all_to_all(x, axis, 0, 0, tiled=True)


def to_all(x, axis, count):
    return exchange(jnp.broadcast_to(x[None], (count,) + x.shape), axis)


def cut_lanes(x, count):
    width = x.shape[1] // count
    return jnp.stack([x[:, i * width : (i + 1) * width] for i in range(count)])


def join_lanes(x):
    return jnp.concatenate([x[i] for i in range(x.shape[0])], axis=1)


def add_up(x):
    total = x[0].astype(F32)
    for i in range(1, x.shape[0]):
        total = total + x[i].astype(F32)
    return total


def all_tokens_of_y(tokens):
    nh, nl = lax.axis_size("zh"), lax.axis_size("zl")
    here, width = tokens.shape
    cut = cut_lanes(tokens, nl)
    cut = jnp.broadcast_to(cut[None], (nh,) + cut.shape).reshape(nh * nl, here, width // nl)
    return exchange(cut, ("zh", "zl")).reshape(nh * nl * here, width // nl)


def gather_routed(held, route_index):
    ny, nl = lax.axis_size("y"), lax.axis_size("zl")
    count, quarter = held.shape
    rows = route_index.shape[0]
    place = route_index - lax.axis_index("y") * count
    pick = (place[:, None] == lax.broadcasted_iota(jnp.int32, (rows, count), 1)).astype(BF)
    filled = jnp.dot(pick, held, preferred_element_type=F32).astype(BF)
    got = add_up(exchange(filled.reshape(ny, rows // ny, quarter), "y")).astype(BF)
    got = join_lanes(to_all(got, "zl", nl))
    return to_all(got, "y", ny).reshape(rows, nl * quarter)


def activate(gate, up, back):
    sig = jax.nn.sigmoid(gate)
    silu = gate * sig
    hidden = (silu * up).astype(BF)
    grad_up = (back * silu).astype(BF)
    grad_gate = (back * up * sig * (1.0 + gate * (1.0 - sig))).astype(BF)
    return (hidden, grad_gate, grad_up)


def chip_sum(part):
    half = part.shape[1] // lax.axis_size("core")
    core = lax.axis_index("core")
    keep = lax.dynamic_slice_in_dim(part, core * half, half, 1)
    give = lax.dynamic_slice_in_dim(part, (1 - core) * half, half, 1)
    return keep + lax.ppermute(give, "core", [(0, 1), (1, 0)])


def sum_by_pairs(part):
    part = part + lax.ppermute(part, "x", [(0, 1), (1, 0), (2, 3), (3, 2)])
    return part + lax.ppermute(part, "x", [(0, 3), (3, 0), (1, 2), (2, 1)])


def scatter_rows(total, out_grad):
    rows, width = total.shape
    ny, nh, nl = lax.axis_size("y"), lax.axis_size("zh"), lax.axis_size("zl")
    slots, quarter = rows // ny, width // nl
    each = slots // (nh * nl)
    part = add_up(exchange(total.reshape(ny, slots, width), "y")).astype(BF)
    part = add_up(exchange(cut_lanes(part, nl), "zl")).astype(BF)
    part = exchange(part.reshape(nh * nl, each, quarter), ("zh", "zl"))
    part = join_lanes(add_up(part.reshape(nh, nl, each, quarter)))
    first = lax.axis_index(("y", "zh", "zl")) * each
    mine = lax.dynamic_slice_in_dim(out_grad, first, each, 0)
    return (mine.astype(F32) + part).astype(BF)


def body(tokens, route_index, router_score, out_grad, gate_weight, up_weight, down_weight):
    units = down_weight.shape[0]
    padded = (units + 15) // 16 * 16
    more = ((0, padded - units), (0, 0))
    both = jnp.concatenate([jnp.pad(gate_weight.T, more), jnp.pad(up_weight.T, more)])
    held = all_tokens_of_y(tokens)
    scaled = (router_score[:, None] * out_grad.astype(F32)).astype(BF)
    back = sum_by_pairs(chip_sum(dot(jnp.pad(down_weight, more), scaled, 1, 1)))
    held, back, both = lax.optimization_barrier((held, back, both))
    routed = gather_routed(held, route_index)
    sums = add_up(to_all(chip_sum(dot(both, routed, 1, 1)).astype(BF), "x", lax.axis_size("x")))
    grads = jnp.stack(activate(sums[:padded], sums[padded:], back))
    grads = lax.all_gather(grads, "core", axis=2, tiled=True)
    total = dot(grads[1:].reshape(2 * padded, -1), both, 0, 0)
    d_rows = scatter_rows(total.astype(BF), out_grad)
    d_down = dot(grads[0, :units], scaled, 1, 0).astype(BF)
    d_gate = dot(routed, grads[1, :units], 0, 1).astype(BF)
    d_up = dot(routed, grads[2, :units], 0, 1).astype(BF)
    return (d_rows, d_gate, d_up, d_down)


def solution(mesh):
    rows, cols = mesh.devices.shape
    fine = Mesh(mesh.devices.reshape(rows // 2, 2, 4, cols // 16, 4), ("x", "core", "y", "zh", "zl"))
    row, col = ("x", "core"), ("y", "zh", "zl")
    placed = (
        P(col, row),
        P(),
        P(),
        P(None, row),
        P(row, col),
        P(row, col),
        P(col, row),
    )
    return jax.shard_map(
        body,
        mesh=fine,
        in_specs=placed,
        out_specs=(P(col, row), P(row, col), P(row, col), P(col, row)),
        check_vma=False,
    )
```

```python
import jax
import jax.numpy as jnp
from jax import lax
from jax.sharding import Mesh
from jax.sharding import PartitionSpec as P

BF = jnp.bfloat16
F32 = jnp.float32
Z = ("za", "zb", "zc")


def dot(a, b, i, j):
    return lax.dot_general(a, b, (((i,), (j,)), ((), ())), preferred_element_type=F32)


def exchange(x, axis):
    return lax.all_to_all(x, axis, 0, 0, tiled=True)


def to_all(x, axis, count):
    return exchange(jnp.broadcast_to(x[None], (count,) + x.shape), axis)


def cut_lanes(x, count):
    rows, width = x.shape
    part = width // count
    return x.reshape(rows // 8, 8, count, part).transpose(2, 0, 1, 3).reshape(count, rows, part)


def join_lanes(x):
    count, rows, part = x.shape
    return x.reshape(count, rows // 8, 8, part).transpose(1, 2, 0, 3).reshape(rows, count * part)


def add_up(x):
    total = x[0].astype(F32)
    for i in range(1, x.shape[0]):
        total = total + x[i].astype(F32)
    return total


def all_tokens_of_y(tokens):
    nh, nl = lax.axis_size("za"), lax.axis_size("zb") * lax.axis_size("zc")
    here, width = tokens.shape
    cut = cut_lanes(tokens, nl)
    cut = jnp.broadcast_to(cut[None], (nh,) + cut.shape).reshape(nh * nl, here, width // nl)
    return exchange(cut, Z).reshape(nh * nl * here, width // nl)


def gather_routed(held, route_index):
    ny, nl = lax.axis_size("y"), lax.axis_size("zb") * lax.axis_size("zc")
    count, share = held.shape
    rows = route_index.shape[0]
    place = route_index - lax.axis_index("y") * count
    pick = (place[:, None] == lax.broadcasted_iota(jnp.int32, (rows, count), 1)).astype(BF)
    filled = jnp.dot(pick, held, preferred_element_type=F32).astype(BF)
    got = add_up(exchange(filled.reshape(ny, rows // ny, share), "y")).astype(BF)
    got = join_lanes(to_all(got, ("zb", "zc"), nl))
    return to_all(got, "y", ny).reshape(rows, nl * share)


def activate(gate, up, back):
    sig = jax.nn.sigmoid(gate)
    silu = gate * sig
    hidden = (silu * up).astype(BF)
    grad_up = (back * silu).astype(BF)
    grad_gate = (back * up * sig * (1.0 + gate * (1.0 - sig))).astype(BF)
    return (hidden, grad_gate, grad_up)


def chip_sum(part):
    half = part.shape[1] // lax.axis_size("core")
    core = lax.axis_index("core")
    keep = lax.dynamic_slice_in_dim(part, core * half, half, 1)
    give = lax.dynamic_slice_in_dim(part, (1 - core) * half, half, 1)
    return keep + lax.ppermute(give, "core", [(0, 1), (1, 0)])


def sum_by_pairs(part):
    part = part + lax.ppermute(part, "x", [(0, 1), (1, 0), (2, 3), (3, 2)])
    return part + lax.ppermute(part, "x", [(0, 3), (3, 0), (1, 2), (2, 1)])


def scatter_rows(total, out_grad):
    rows, width = total.shape
    ny, nh, nl = lax.axis_size("y"), lax.axis_size("za") * lax.axis_size("zb"), lax.axis_size("zc")
    slots, quarter = rows // ny, width // nl
    each = slots // (nh * nl)
    part = add_up(exchange(total.reshape(ny, slots, width), "y")).astype(BF)
    part = jnp.stack([part[:, i * quarter : (i + 1) * quarter] for i in range(nl)])
    part = add_up(exchange(part, "zc")).astype(BF)
    part = exchange(part.reshape(nh * nl, each, quarter), Z)
    part = add_up(part.reshape(nh, nl, each, quarter)).transpose(1, 0, 2).reshape(each, width)
    first = lax.axis_index(("y",) + Z) * each
    mine = lax.dynamic_slice_in_dim(out_grad, first, each, 0)
    return (mine.astype(F32) + part).astype(BF)


def body(tokens, route_index, router_score, out_grad, gate_weight, up_weight, down_weight):
    units = down_weight.shape[0]
    padded = (units + 15) // 16 * 16
    more = ((0, padded - units), (0, 0))
    both = jnp.concatenate([jnp.pad(gate_weight.T, more), jnp.pad(up_weight.T, more)])
    held = all_tokens_of_y(tokens)
    scaled = (router_score[:, None] * out_grad.astype(F32)).astype(BF)
    back = sum_by_pairs(chip_sum(dot(jnp.pad(down_weight, more), scaled, 1, 1)))
    held, back, both = lax.optimization_barrier((held, back, both))
    routed = gather_routed(held, route_index)
    sums = add_up(to_all(chip_sum(dot(both, routed, 1, 1)).astype(BF), "x", lax.axis_size("x")))
    grads = jnp.stack(activate(sums[:padded], sums[padded:], back))
    grads = lax.all_gather(grads, "core", axis=2, tiled=True)
    total = dot(grads[1:].reshape(2 * padded, -1), both, 0, 0)
    d_rows = scatter_rows(total.astype(BF), out_grad)
    d_down = dot(grads[0, :units], scaled, 1, 0).astype(BF)
    d_gate = dot(routed, grads[1, :units], 0, 1).astype(BF)
    d_up = dot(routed, grads[2, :units], 0, 1).astype(BF)
    return (d_rows, d_gate, d_up, d_down)


def solution(mesh):
    rows, cols = mesh.devices.shape
    fine = Mesh(mesh.devices.reshape(rows // 2, 2, 4, cols // 32, 2, 4), ("x", "core", "y") + Z)
    row, col = ("x", "core"), ("y",) + Z
    placed = (
        P(col, row),
        P(),
        P(),
        P(None, row),
        P(row, col),
        P(row, col),
        P(col, row),
    )
    return jax.shard_map(
        body,
        mesh=fine,
        in_specs=placed,
        out_specs=(P(col, row), P(row, col), P(row, col), P(col, row)),
        check_vma=False,
    )
```

```python
import jax
import jax.numpy as jnp
from jax import lax
from jax.sharding import Mesh
from jax.sharding import PartitionSpec as P

BF = jnp.bfloat16
F32 = jnp.float32
NEAR = 4


def dot(a, b, i, j):
    return lax.dot_general(a, b, (((i,), (j,)), ((), ())), preferred_element_type=F32)


def exchange(x, axis, groups=None):
    return lax.all_to_all(x, axis, 0, 0, tiled=True, axis_index_groups=groups)


def to_all(x, axis, count, groups=None):
    return exchange(jnp.broadcast_to(x[None], (count,) + x.shape), axis, groups)


def near(nz):
    return [list(range(i, i + NEAR)) for i in range(0, nz, NEAR)]


def ring(nz):
    return [[(i + nz // 2) % nz for i in range(nz)]]


def cut_lanes(x, count):
    width = x.shape[1] // count
    return jnp.stack([x[:, i * width : (i + 1) * width] for i in range(count)])


def join_lanes(x):
    return jnp.concatenate([x[i] for i in range(x.shape[0])], axis=1)


def add_up(x):
    total = x[0].astype(F32)
    for i in range(1, x.shape[0]):
        total = total + x[i].astype(F32)
    return total


def all_tokens_of_y(tokens):
    nz = lax.axis_size("z")
    here, width = tokens.shape
    cut = cut_lanes(tokens, NEAR)
    cut = jnp.broadcast_to(cut[None], (nz // NEAR,) + cut.shape).reshape(nz, here, width // NEAR)
    return exchange(cut, "z", ring(nz)).reshape(nz * here, width // NEAR)


def gather_routed(held, route_index):
    ny, nz = lax.axis_size("y"), lax.axis_size("z")
    count, part = held.shape
    rows = route_index.shape[0]
    place = route_index - lax.axis_index("y") * count
    held_at = jnp.where(place < count // 2, place + count // 2, place - count // 2)
    place = jnp.where((place >= 0) & (place < count), held_at, -1)
    pick = (place[:, None] == lax.broadcasted_iota(jnp.int32, (rows, count), 1)).astype(BF)
    filled = jnp.dot(pick, held, preferred_element_type=F32).astype(BF)
    got = add_up(exchange(filled.reshape(ny, rows // ny, part), "y")).astype(BF)
    got = join_lanes(to_all(got, "z", NEAR, near(nz)))
    return to_all(got, "y", ny).reshape(rows, NEAR * part)


def activate(gate, up, back):
    sig = jax.nn.sigmoid(gate)
    silu = gate * sig
    hidden = (silu * up).astype(BF)
    grad_up = (back * silu).astype(BF)
    grad_gate = (back * up * sig * (1.0 + gate * (1.0 - sig))).astype(BF)
    return (hidden, grad_gate, grad_up)


def chip_sum(part):
    half = part.shape[1] // lax.axis_size("core")
    core = lax.axis_index("core")
    keep = lax.dynamic_slice_in_dim(part, core * half, half, 1)
    give = lax.dynamic_slice_in_dim(part, (1 - core) * half, half, 1)
    return keep + lax.ppermute(give, "core", [(0, 1), (1, 0)])


def sum_by_pairs(part):
    part = part + lax.ppermute(part, "x", [(0, 1), (1, 0), (2, 3), (3, 2)])
    return part + lax.ppermute(part, "x", [(0, 3), (3, 0), (1, 2), (2, 1)])


def scatter_rows(total, out_grad):
    rows, width = total.shape
    ny, nz = lax.axis_size("y"), lax.axis_size("z")
    slots, quarter = rows // ny, width // NEAR
    each = slots // nz
    part = add_up(exchange(total.reshape(ny, slots, width), "y")).astype(BF)
    part = add_up(exchange(cut_lanes(part, NEAR), "z", near(nz))).astype(BF)
    part = jnp.concatenate([part[slots // 2 :], part[: slots // 2]])
    part = exchange(part.reshape(nz, each, quarter), "z", ring(nz))
    part = join_lanes(add_up(part.reshape(nz // NEAR, NEAR, each, quarter)))
    first = lax.axis_index(("y", "z")) * each
    mine = lax.dynamic_slice_in_dim(out_grad, first, each, 0)
    return (mine.astype(F32) + part).astype(BF)


def body(tokens, route_index, router_score, out_grad, gate_weight, up_weight, down_weight):
    units = down_weight.shape[0]
    padded = (units + 15) // 16 * 16
    more = ((0, padded - units), (0, 0))
    both = jnp.concatenate([jnp.pad(gate_weight.T, more), jnp.pad(up_weight.T, more)])
    held = all_tokens_of_y(tokens)
    scaled = (router_score[:, None] * out_grad.astype(F32)).astype(BF)
    back = sum_by_pairs(chip_sum(dot(jnp.pad(down_weight, more), scaled, 1, 1)))
    held, back, both = lax.optimization_barrier((held, back, both))
    routed = gather_routed(held, route_index)
    sums = add_up(to_all(chip_sum(dot(both, routed, 1, 1)).astype(BF), "x", lax.axis_size("x")))
    grads = jnp.stack(activate(sums[:padded], sums[padded:], back))
    grads = lax.all_gather(grads, "core", axis=2, tiled=True)
    total = dot(grads[1:].reshape(2 * padded, -1), both, 0, 0)
    d_rows = scatter_rows(total.astype(BF), out_grad)
    d_down = dot(grads[0, :units], scaled, 1, 0).astype(BF)
    d_gate = dot(routed, grads[1, :units], 0, 1).astype(BF)
    d_up = dot(routed, grads[2, :units], 0, 1).astype(BF)
    return (d_rows, d_gate, d_up, d_down)


def solution(mesh):
    rows, cols = mesh.devices.shape
    fine = Mesh(mesh.devices.reshape(rows // 2, 2, 4, cols // 4), ("x", "core", "y", "z"))
    row, col = ("x", "core"), ("y", "z")
    placed = (
        P(col, row),
        P(),
        P(),
        P(None, row),
        P(row, col),
        P(row, col),
        P(col, row),
    )
    return jax.shard_map(
        body,
        mesh=fine,
        in_specs=placed,
        out_specs=(P(col, row), P(row, col), P(row, col), P(col, row)),
        check_vma=False,
    )
```

```python
import jax
import jax.numpy as jnp
from jax import lax
from jax.sharding import Mesh
from jax.sharding import PartitionSpec as P

BF = jnp.bfloat16
F32 = jnp.float32
PARTS = 8
NEAR = 4


def dot(a, b, i, j):
    return lax.dot_general(a, b, (((i,), (j,)), ((), ())), preferred_element_type=F32)


def exchange(x, axis, groups=None):
    return lax.all_to_all(x, axis, 0, 0, tiled=True, axis_index_groups=groups)


def to_all(x, axis, count, groups=None):
    return exchange(jnp.broadcast_to(x[None], (count,) + x.shape), axis, groups)


def near(nz, count):
    order = [(i + count // 2) % count for i in range(count)]
    return [[i + j for j in order] for i in range(0, nz, count)]


def ring_start(nz, count):
    return 5 * nz // 8 // count * count + count // 2


def ring(nz, count):
    return [[(i + ring_start(nz, count)) % nz for i in range(nz)]]


def cut_lanes(x, count):
    rows, width = x.shape
    part = width // count
    return x.reshape(rows // 8, 8, count, part).transpose(2, 0, 1, 3).reshape(count, rows, part)


def join_lanes(x):
    count, rows, part = x.shape
    return x.reshape(count, rows // 8, 8, part).transpose(1, 2, 0, 3).reshape(rows, count * part)


def add_up(x):
    total = x[0].astype(F32)
    for i in range(1, x.shape[0]):
        total = total + x[i].astype(F32)
    return total


def all_tokens_of_y(tokens):
    nz = lax.axis_size("z")
    here, width = tokens.shape
    cut = cut_lanes(tokens, PARTS)
    cut = jnp.broadcast_to(cut[None], (nz // PARTS,) + cut.shape).reshape(nz, here, width // PARTS)
    return exchange(cut, "z", ring(nz, PARTS)).reshape(nz * here, width // PARTS)


def gather_routed(held, route_index):
    ny, nz = lax.axis_size("y"), lax.axis_size("z")
    count, part = held.shape
    rows = route_index.shape[0]
    place = route_index - lax.axis_index("y") * count
    first = ring_start(nz, PARTS) * (count // nz)
    held_at = jnp.where(place < first, place + (count - first), place - first)
    place = jnp.where((place >= 0) & (place < count), held_at, -1)
    pick = (place[:, None] == lax.broadcasted_iota(jnp.int32, (rows, count), 1)).astype(BF)
    filled = jnp.dot(pick, held, preferred_element_type=F32).astype(BF)
    got = add_up(exchange(filled.reshape(ny, rows // ny, part), "y")).astype(BF)
    got = join_lanes(to_all(got, "z", PARTS, near(nz, PARTS)))
    return to_all(got, "y", ny).reshape(rows, PARTS * part)


def activate(gate, up, back):
    sig = jax.nn.sigmoid(gate)
    silu = gate * sig
    hidden = (silu * up).astype(BF)
    grad_up = (back * silu).astype(BF)
    grad_gate = (back * up * sig * (1.0 + gate * (1.0 - sig))).astype(BF)
    return (hidden, grad_gate, grad_up)


def chip_sum(part):
    half = part.shape[1] // lax.axis_size("core")
    core = lax.axis_index("core")
    keep = lax.dynamic_slice_in_dim(part, core * half, half, 1)
    give = lax.dynamic_slice_in_dim(part, (1 - core) * half, half, 1)
    return keep + lax.ppermute(give, "core", [(0, 1), (1, 0)])


def sum_by_pairs(part):
    part = part + lax.ppermute(part, "x", [(0, 1), (1, 0), (2, 3), (3, 2)])
    return part + lax.ppermute(part, "x", [(0, 3), (3, 0), (1, 2), (2, 1)])


def scatter_rows(total, out_grad):
    rows, width = total.shape
    ny, nz = lax.axis_size("y"), lax.axis_size("z")
    slots, quarter = rows // ny, width // NEAR
    each = slots // nz
    part = add_up(exchange(total.reshape(ny, slots, width), "y")).astype(BF)
    part = jnp.stack([part[:, i * quarter : (i + 1) * quarter] for i in range(NEAR)])
    part = exchange(part, "z", near(nz, NEAR))
    turn = ring_start(nz, NEAR) * each
    part = jnp.concatenate([add_up(part[:, turn:]), add_up(part[:, :turn])]).astype(BF)
    part = exchange(part.reshape(nz, each, quarter), "z", ring(nz, NEAR))
    part = add_up(part.reshape(nz // NEAR, NEAR, each, quarter)).transpose(1, 0, 2).reshape(each, width)
    first = lax.axis_index(("y", "z")) * each
    mine = lax.dynamic_slice_in_dim(out_grad, first, each, 0)
    return (mine.astype(F32) + part).astype(BF)


def body(tokens, route_index, router_score, out_grad, gate_weight, up_weight, down_weight):
    units = down_weight.shape[0]
    padded = (units + 15) // 16 * 16
    more = ((0, padded - units), (0, 0))
    both = jnp.concatenate([jnp.pad(gate_weight.T, more), jnp.pad(up_weight.T, more)])
    held = all_tokens_of_y(tokens)
    scaled = (router_score[:, None] * out_grad.astype(F32)).astype(BF)
    back = sum_by_pairs(chip_sum(dot(jnp.pad(down_weight, more), scaled, 1, 1)))
    held, back, both = lax.optimization_barrier((held, back, both))
    routed = gather_routed(held, route_index)
    sums = add_up(to_all(chip_sum(dot(both, routed, 1, 1)).astype(BF), "x", lax.axis_size("x")))
    grads = jnp.stack(activate(sums[:padded], sums[padded:], back))
    grads = lax.all_gather(grads, "core", axis=2, tiled=True)
    total = dot(grads[1:].reshape(2 * padded, -1), both, 0, 0)
    d_rows = scatter_rows(total.astype(BF), out_grad)
    d_down = dot(grads[0, :units], scaled, 1, 0).astype(BF)
    d_gate = dot(routed, grads[1, :units], 0, 1).astype(BF)
    d_up = dot(routed, grads[2, :units], 0, 1).astype(BF)
    return (d_rows, d_gate, d_up, d_down)


def solution(mesh):
    rows, cols = mesh.devices.shape
    fine = Mesh(mesh.devices.reshape(rows // 2, 2, 4, cols // 4), ("x", "core", "y", "z"))
    row, col = ("x", "core"), ("y", "z")
    placed = (
        P(col, row),
        P(),
        P(),
        P(None, row),
        P(row, col),
        P(row, col),
        P(col, row),
    )
    return jax.shard_map(
        body,
        mesh=fine,
        in_specs=placed,
        out_specs=(P(col, row), P(row, col), P(row, col), P(col, row)),
        check_vma=False,
    )
```

```python
import jax
import jax.numpy as jnp
from jax import lax
from jax.sharding import Mesh
from jax.sharding import PartitionSpec as P

BF = jnp.bfloat16
F32 = jnp.float32
PARTS = 8
NEAR = 4


def dot(a, b, i, j):
    return lax.dot_general(a, b, (((i,), (j,)), ((), ())), preferred_element_type=F32)


def exchange(x, axis, groups=None):
    return lax.all_to_all(x, axis, 0, 0, tiled=True, axis_index_groups=groups)


def to_all(x, axis, count, groups=None):
    return exchange(jnp.broadcast_to(x[None], (count,) + x.shape), axis, groups)


def near(nz, count, turn):
    order = [(i + turn) % count for i in range(count)]
    return [[i + j for j in order] for i in range(0, nz, count)]


def ring(nz, turn):
    return [[(i + turn) % nz for i in range(nz)]]


def cut_lanes(x, count):
    rows, width = x.shape
    part = width // count
    return x.reshape(rows // 8, 8, count, part).transpose(2, 0, 1, 3).reshape(count, rows, part)


def join_lanes(x):
    count, rows, part = x.shape
    return x.reshape(count, rows // 8, 8, part).transpose(1, 2, 0, 3).reshape(rows, count * part)


def add_up(x):
    total = x[0].astype(F32)
    for i in range(1, x.shape[0]):
        total = total + x[i].astype(F32)
    return total


def all_tokens_of_y(tokens):
    nz = lax.axis_size("z")
    here, width = tokens.shape
    cut = cut_lanes(tokens, PARTS)
    cut = jnp.broadcast_to(cut[None], (nz // PARTS,) + cut.shape).reshape(nz, here, width // PARTS)
    return exchange(cut, "z", ring(nz, 5 * nz // 8)).reshape(nz * here, width // PARTS)


def share_slots(held, route_index):
    ny, nz = lax.axis_size("y"), lax.axis_size("z")
    count, part = held.shape
    rows = route_index.shape[0]
    place = route_index - lax.axis_index("y") * count
    turn = 5 * nz // 8
    first = turn * (count // nz)
    held_at = jnp.where(place < first, place + (count - first), place - first)
    place = jnp.where((place >= 0) & (place < count), held_at, -1)
    pick = (place[:, None] == lax.broadcasted_iota(jnp.int32, (rows, count), 1)).astype(BF)
    filled = jnp.dot(pick, held, preferred_element_type=F32).astype(BF)
    got = add_up(exchange(filled.reshape(ny, rows // ny, part), "y")).astype(BF)
    return to_all(got, "z", PARTS, near(nz, PARTS, turn % PARTS))


def activate(gate, up, back):
    sig = jax.nn.sigmoid(gate)
    silu = gate * sig
    hidden = (silu * up).astype(BF)
    grad_up = (back * silu).astype(BF)
    grad_gate = (back * up * sig * (1.0 + gate * (1.0 - sig))).astype(BF)
    return (hidden, grad_gate, grad_up)


def chip_sum(part):
    half = part.shape[1] // lax.axis_size("core")
    core = lax.axis_index("core")
    keep = lax.dynamic_slice_in_dim(part, core * half, half, 1)
    give = lax.dynamic_slice_in_dim(part, (1 - core) * half, half, 1)
    return keep + lax.ppermute(give, "core", [(0, 1), (1, 0)])


def add_neighbour(part, turn):
    nx = lax.axis_size("x")
    pairs = [((i + turn) % nx, ((i ^ 1) + turn) % nx) for i in range(nx)]
    return part + lax.ppermute(part, "x", pairs)


def scatter_rows(total, out_grad):
    rows, width = total.shape
    ny, nz = lax.axis_size("y"), lax.axis_size("z")
    slots, quarter = rows // ny, width // NEAR
    each = slots // nz
    part = add_up(exchange(total.reshape(ny, slots, width), "y")).astype(BF)
    part = jnp.stack([part[:, i * quarter : (i + 1) * quarter] for i in range(NEAR)])
    part = exchange(part, "z", near(nz, NEAR, 0))
    turn = nz // 2
    first = turn * each
    part = jnp.concatenate([add_up(part[:, first:]), add_up(part[:, :first])]).astype(BF)
    part = exchange(part.reshape(nz, each, quarter), "z", ring(nz, turn))
    part = add_up(part.reshape(nz // NEAR, NEAR, each, quarter)).transpose(1, 0, 2).reshape(each, width)
    first = lax.axis_index(("y", "z")) * each
    mine = lax.dynamic_slice_in_dim(out_grad, first, each, 0)
    return (mine.astype(F32) + part).astype(BF)


def body(tokens, route_index, router_score, out_grad, gate_weight, up_weight, down_weight):
    units = down_weight.shape[0]
    padded = (units + 15) // 16 * 16
    more = ((0, padded - units), (0, 0))
    both = jnp.concatenate([jnp.pad(gate_weight.T, more), jnp.pad(up_weight.T, more)])
    held = all_tokens_of_y(tokens)
    scaled = (router_score[:, None] * out_grad.astype(F32)).astype(BF)
    back = add_neighbour(chip_sum(dot(jnp.pad(down_weight, more), scaled, 1, 1)), 0)
    held, back, both = lax.optimization_barrier((held, back, both))
    slots = share_slots(held, route_index)
    back = add_neighbour(back, 1)
    slots, back = lax.optimization_barrier((slots, back))
    ny = lax.axis_size("y")
    routed = to_all(join_lanes(slots), "y", ny).reshape(route_index.shape[0], -1)
    sums = add_up(to_all(chip_sum(dot(both, routed, 1, 1)).astype(BF), "x", lax.axis_size("x")))
    grads = jnp.stack(activate(sums[:padded], sums[padded:], back))
    grads = lax.all_gather(grads, "core", axis=2, tiled=True)
    total = dot(grads[1:].reshape(2 * padded, -1), both, 0, 0)
    d_rows = scatter_rows(total.astype(BF), out_grad)
    d_down = dot(grads[0, :units], scaled, 1, 0).astype(BF)
    d_gate = dot(routed, grads[1, :units], 0, 1).astype(BF)
    d_up = dot(routed, grads[2, :units], 0, 1).astype(BF)
    return (d_rows, d_gate, d_up, d_down)


def solution(mesh):
    rows, cols = mesh.devices.shape
    fine = Mesh(mesh.devices.reshape(rows // 2, 2, 4, cols // 4), ("x", "core", "y", "z"))
    row, col = ("x", "core"), ("y", "z")
    placed = (
        P(col, row),
        P(),
        P(),
        P(None, row),
        P(row, col),
        P(row, col),
        P(col, row),
    )
    return jax.shard_map(
        body,
        mesh=fine,
        in_specs=placed,
        out_specs=(P(col, row), P(row, col), P(row, col), P(col, row)),
        check_vma=False,
    )
```

```python
import jax
import jax.numpy as jnp
from jax import lax
from jax.sharding import Mesh
from jax.sharding import PartitionSpec as P

BF = jnp.bfloat16
F32 = jnp.float32
PARTS = 8
NEAR = 4


def dot(a, b, i, j):
    return lax.dot_general(a, b, (((i,), (j,)), ((), ())), preferred_element_type=F32)


def exchange(x, axis, groups=None):
    return lax.all_to_all(x, axis, 0, 0, tiled=True, axis_index_groups=groups)


def to_all(x, axis, count, groups=None):
    return exchange(jnp.broadcast_to(x[None], (count,) + x.shape), axis, groups)


def near(nz, count, turn):
    order = [(i + turn) % count for i in range(count)]
    return [[i + j for j in order] for i in range(0, nz, count)]


def ring(nz, turn):
    return [[(i + turn) % nz for i in range(nz)]]


def cut_lanes(x, count):
    rows, width = x.shape
    part = width // count
    return x.reshape(rows // 8, 8, count, part).transpose(2, 0, 1, 3).reshape(count, rows, part)


def join_lanes(x):
    count, rows, part = x.shape
    return x.reshape(count, rows // 8, 8, part).transpose(1, 2, 0, 3).reshape(rows, count * part)


def add_up(x):
    total = x[0].astype(F32)
    for i in range(1, x.shape[0]):
        total = total + x[i].astype(F32)
    return total


def all_tokens_of_y(tokens):
    nz = lax.axis_size("z")
    here, width = tokens.shape
    cut = cut_lanes(tokens, PARTS)
    cut = jnp.broadcast_to(cut[None], (nz // PARTS,) + cut.shape).reshape(nz, here, width // PARTS)
    return exchange(cut, "z", ring(nz, 5 * nz // 8)).reshape(nz * here, width // PARTS)


def share_slots(held, route_index):
    ny, nz = lax.axis_size("y"), lax.axis_size("z")
    count, part = held.shape
    rows = route_index.shape[0]
    place = route_index - lax.axis_index("y") * count
    turn = 5 * nz // 8
    first = turn * (count // nz)
    held_at = jnp.where(place < first, place + (count - first), place - first)
    place = jnp.where((place >= 0) & (place < count), held_at, -1)
    pick = (place[:, None] == lax.broadcasted_iota(jnp.int32, (rows, count), 1)).astype(BF)
    filled = jnp.dot(pick, held, preferred_element_type=F32).astype(BF)
    got = add_up(exchange(filled.reshape(ny, rows // ny, part), "y")).astype(BF)
    return to_all(got, "z", PARTS, near(nz, PARTS, turn % PARTS))


def activate(gate, up, back):
    sig = jax.nn.sigmoid(gate)
    silu = gate * sig
    hidden = (silu * up).astype(BF)
    grad_up = (back * silu).astype(BF)
    grad_gate = (back * up * sig * (1.0 + gate * (1.0 - sig))).astype(BF)
    return (hidden, grad_gate, grad_up)


def chip_sum(part):
    half = part.shape[1] // lax.axis_size("core")
    core = lax.axis_index("core")
    keep = lax.dynamic_slice_in_dim(part, core * half, half, 1)
    give = lax.dynamic_slice_in_dim(part, (1 - core) * half, half, 1)
    return keep + lax.ppermute(give, "core", [(0, 1), (1, 0)])


def add_neighbour(part, turn):
    nx = lax.axis_size("x")
    pairs = [((i + turn) % nx, ((i ^ 1) + turn) % nx) for i in range(nx)]
    return part + lax.ppermute(part, "x", pairs)


def scatter_rows(total, out_grad):
    rows, width = total.shape
    ny, nz = lax.axis_size("y"), lax.axis_size("z")
    slots, quarter = rows // ny, width // NEAR
    each = slots // nz
    part = add_up(exchange(total.reshape(ny, slots, width), "y")).astype(BF)
    part = jnp.stack([part[:, i * quarter : (i + 1) * quarter] for i in range(NEAR)])
    part = exchange(part, "z", near(nz, NEAR, 0))
    turn = 3 * nz // 4
    first = turn * each
    part = jnp.concatenate([add_up(part[:, first:]), add_up(part[:, :first])]).astype(BF)
    part = exchange(part.reshape(nz, each, quarter), "z", ring(nz, turn))
    part = add_up(part.reshape(nz // NEAR, NEAR, each, quarter)).transpose(1, 0, 2).reshape(each, width)
    first = lax.axis_index(("y", "z")) * each
    mine = lax.dynamic_slice_in_dim(out_grad, first, each, 0)
    return (mine.astype(F32) + part).astype(BF)


def body(tokens, route_index, router_score, out_grad, gate_weight, up_weight, down_weight):
    units = down_weight.shape[0]
    padded = (units + 15) // 16 * 16
    more = ((0, padded - units), (0, 0))
    both = jnp.concatenate([jnp.pad(gate_weight.T, more), jnp.pad(up_weight.T, more)])
    held = all_tokens_of_y(tokens)
    scaled = (router_score[:, None] * out_grad.astype(F32)).astype(BF)
    back = add_neighbour(chip_sum(dot(jnp.pad(down_weight, more), scaled, 1, 1)), 0)
    held, back, both = lax.optimization_barrier((held, back, both))
    slots = share_slots(held, route_index)
    back = add_neighbour(back, 1)
    slots, back = lax.optimization_barrier((slots, back))
    ny = lax.axis_size("y")
    routed = to_all(join_lanes(slots), "y", ny).reshape(route_index.shape[0], -1)
    sums = add_up(to_all(chip_sum(dot(both, routed, 1, 1)).astype(BF), "x", lax.axis_size("x")))
    grads = jnp.stack(activate(sums[:padded], sums[padded:], back))
    grads = lax.all_gather(grads, "core", axis=2, tiled=True)
    total = dot(grads[1:].reshape(2 * padded, -1), both, 0, 0)
    d_rows = scatter_rows(total.astype(BF), out_grad)
    d_down = dot(grads[0, :units], scaled, 1, 0).astype(BF)
    d_gate = dot(routed, grads[1, :units], 0, 1).astype(BF)
    d_up = dot(routed, grads[2, :units], 0, 1).astype(BF)
    return (d_rows, d_gate, d_up, d_down)


def solution(mesh):
    rows, cols = mesh.devices.shape
    fine = Mesh(mesh.devices.reshape(rows // 2, 2, 4, cols // 4), ("x", "core", "y", "z"))
    row, col = ("x", "core"), ("y", "z")
    placed = (
        P(col, row),
        P(),
        P(),
        P(None, row),
        P(row, col),
        P(row, col),
        P(col, row),
    )
    return jax.shard_map(
        body,
        mesh=fine,
        in_specs=placed,
        out_specs=(P(col, row), P(row, col), P(row, col), P(col, row)),
        check_vma=False,
    )
```
